256 devices in a mesh: section: 16 (over z, core), dp: 16 (over y, x).
Axes of the slice: x: 4, y: 4, z: 8, core: 2. Of those that a mesh axis runs over, the one named last changes fastest.
Arguments:
- layer_inputs: bfloat16 [16, 16, 1024, 4096], P('section', 'dp'), may hold values from -2.5 to 2.5
- keys_values: bfloat16 [16, 16, 1024, 1024], P('section', 'dp'), may hold values from -2.5 to 2.5
- loss_weight: float32 [16, 1024], P('dp'), may hold values from 0.25 to 4
- doc_ids: int32 [16, 8, 128], replicated, may hold values from 0 to 3, never falling along the last dimension, each value on 1 to 64 neighbouring positions
- assignment: int32 [16, 8], replicated, may hold values from 0 to 15, as said below
Outputs:
- key_value_grads: bfloat16 [16, 16, 1024, 1024], P('section', 'dp')
The draws below stay inside these ranges and needn't reach their ends.
Inputs may be any that keep to these rules, and one draw needn't show every extreme that they name: For every microbatch m the column assignment[:, m] is a permutation of the replicas, and no replica hands more than 1 of its microbatches to one replica. `doc_ids`: within a microbatch the ids never fall; a document has at most 64 positions.
All inputs are finite; a program needn't handle non-finite values.
Results may differ from the reference program's by a relative error of at most 0.0097.
Values may be sent and summed in bfloat16 or wider, within the bound.
A program may use at most 128 MiB of HBM per device.

```python
import math
import jax
import jax.numpy as jnp
import numpy as np
from jax import lax

KV_HEADS = 4
HEAD_DIM = 128
SEQ = 128
MICRO = 8
LAYERS = 16
REPLICAS = 16
FEATURES = 4096
KVF = 1024
TOKDEV = 1024


def draw_assignment(key, part):
    key = jax.random.fold_in(key, 7)
    key_turns, key_micro, key_label = jax.random.split(key, 3)
    replica_turn = jax.random.permutation(key_turns, REPLICAS)
    micro_turn = jax.random.permutation(key_micro, MICRO)
    relabel = jax.random.permutation(key_label, REPLICAS)
    slot_index = (replica_turn[:, None] + micro_turn[None, :]) % REPLICAS
    return relabel[slot_index].astype(jnp.int32)


def levels(rng, extent, pieces, low, high):
    def one(position, blocks):
        heights = jax.random.uniform(jax.random.fold_in(jax.random.fold_in(rng, 6), position), (blocks,), jnp.float32, low / len(pieces), high / len(pieces))
        return jnp.repeat(jnp.exp(heights), extent[position] // blocks).reshape((-1,) + (1,) * (len(extent) - position - 1))

    loudness = one(*pieces[0])
    for cut in pieces[1:]:
        loudness = loudness * one(*cut)
    return loudness


def profile(count, total, most, slope):
    weights = [(1 << 20) // math.isqrt(grade ** slope) + 1 for grade in range(2, count + 1)]
    surplus, counts = total - most - (count - 1), [1] * (count - 1)
    while surplus > 0:
        free = [i for i in range(count - 1) if counts[i] < most]
        mass, budget = sum([weights[i] for i in free]), surplus
        for i in free:
            more = min(most - counts[i], max(1, budget * weights[i] // mass), surplus)
            counts[i] = counts[i] + more
            surplus = surplus - more
    return np.array([most] + counts)


def ragged_sizes(stream_key, amount, total, reach, skew):
    if amount == 2:
        one = jax.random.randint(stream_key, (), max(1, total - reach), min(reach, total - 1) + 1)
        return jnp.stack([one, total - one])
    lengths = jnp.asarray(profile(amount, total, reach, skew), jnp.int32)
    couples = (amount - 1) // 2
    giver, receiver = lengths[1:1 + 2 * couples:2], lengths[2:2 + 2 * couples:2]
    room = jnp.minimum(giver - 1, reach - receiver)
    moved = jax.random.randint(jax.random.fold_in(stream_key, 1), (couples,), 0, 1 << 20) % (room + 1)
    lengths = lengths.at[1:1 + 2 * couples:2].set(giver - moved).at[2:2 + 2 * couples:2].set(receiver + moved)
    return lengths[jax.random.permutation(jax.random.fold_in(stream_key, 2), amount)]


def noise(stream_key, shape, scale, bound, cuts=(), held_as=jnp.bfloat16):
    entries = jax.random.normal(stream_key, shape, jnp.float32) * scale
    if len(cuts) > 0:
        entries = levels(stream_key, shape, cuts, -0.22, 0.18) * entries
    return jnp.clip(entries, min=-bound, max=bound).astype(held_as)


def setup_inputs(seed: int = 0) -> dict:
    streams_of = jax.random.split(jax.random.key(seed), 6)
    return {
        "layer_inputs": noise(streams_of[0], (LAYERS, REPLICAS, TOKDEV, FEATURES), 1.0, 2.5, ((0, 16), (1, 16))),
        "keys_values": noise(streams_of[1], (LAYERS, REPLICAS, TOKDEV, KVF), 1.0, 2.5, ((0, 16), (1, 16))),
        "loss_weight": jnp.clip(jnp.exp(math.log(4.0) - 2.7725887 * jax.random.uniform(streams_of[2], (REPLICAS, TOKDEV), jnp.float32) ** levels(streams_of[2], (REPLICAS, TOKDEV), ((0, 16),), -0.2, 0.2)), 0.25, 4.0),
        "doc_ids": jax.vmap(lambda own: jnp.searchsorted(jnp.cumsum(ragged_sizes(own, 4, SEQ, SEQ // 2, 1)), jnp.arange(SEQ), side="right"))(jax.random.split(streams_of[3], REPLICAS * MICRO)).reshape((REPLICAS, MICRO, SEQ)).astype(jnp.int32),
        "assignment": draw_assignment(jax.random.fold_in(streams_of[5], 71), 0),
    }


def source_of(assignment, worker):
    replica_ids = jnp.arange(assignment.shape[0], dtype=jnp.int32)
    return lax.optimization_barrier(jnp.sum(jnp.where(assignment == worker, replica_ids[:, None], 0), axis=0)).astype(jnp.int32)

def mask_of(documents):
    positions = jnp.arange(documents.shape[0], dtype=jnp.int32)
    return (documents[:, None] == documents[None, :]) & (positions[None, :] <= positions[:, None])

def heads_of(queries, gathered):
    query_heads = queries.astype(jnp.float32).reshape(queries.shape[0], KV_HEADS, -1, HEAD_DIM)
    key_heads = gathered[:, :KV_HEADS * HEAD_DIM].astype(jnp.float32).reshape(-1, KV_HEADS, HEAD_DIM)
    value_heads = gathered[:, KV_HEADS * HEAD_DIM:].astype(jnp.float32).reshape(-1, KV_HEADS, HEAD_DIM)
    return (query_heads, key_heads, value_heads)

def attention_weights(query_heads, key_heads, allowed):
    scores = jnp.einsum('ikgd,jkd->kgij', query_heads, key_heads, precision=lax.Precision.HIGHEST) * HEAD_DIM ** (-0.5)
    soft = jnp.where(allowed[None, None], jnp.exp(scores), 0.0)
    return soft / lax.optimization_barrier(jnp.sum(soft, axis=-1, keepdims=True))

def top_grad(queries, gathered, allowed, weights):
    query_heads, key_heads, value_heads = heads_of(queries, gathered)
    soft_weights = attention_weights(query_heads, key_heads, allowed)
    rounded = lax.optimization_barrier(soft_weights.astype(jnp.bfloat16)).astype(jnp.float32)
    mixed_out = jnp.einsum('kgij,jkd->ikgd', rounded, value_heads, precision=lax.Precision.HIGHEST)
    output_sum = queries.astype(jnp.float32) + mixed_out.reshape(queries.shape[0], -1)
    return (weights[:, None] * output_sum).astype(jnp.bfloat16)

def tile_backward(queries, gathered, allowed, upstream):
    query_heads, key_heads, value_heads = heads_of(queries, gathered)
    soft_weights = attention_weights(query_heads, key_heads, allowed)
    grad_heads = upstream.astype(jnp.float32).reshape(upstream.shape[0], KV_HEADS, -1, HEAD_DIM)
    dprobs = jnp.einsum('ikgd,jkd->kgij', grad_heads, value_heads, precision=lax.Precision.HIGHEST)
    row_delta = lax.optimization_barrier(jnp.sum(soft_weights * dprobs, axis=-1, keepdims=True))
    dscores = lax.optimization_barrier((soft_weights * (dprobs - row_delta)).astype(jnp.bfloat16)).astype(jnp.float32)
    rounded = lax.optimization_barrier(soft_weights.astype(jnp.bfloat16)).astype(jnp.float32)
    score_scale = HEAD_DIM ** (-0.5)
    dquery = jnp.einsum('kgij,jkd->ikgd', dscores, key_heads, precision=lax.Precision.HIGHEST) * score_scale
    key_grad = jnp.einsum('kgij,ikgd->jkd', dscores, query_heads, precision=lax.Precision.HIGHEST) * score_scale
    value_grad = jnp.einsum('kgij,ikgd->jkd', rounded, grad_heads, precision=lax.Precision.HIGHEST)
    key_rows = gathered.shape[0]
    key_terms = jnp.concatenate([key_grad.reshape(key_rows, -1), value_grad.reshape(key_rows, -1)], axis=-1)
    return (dquery.reshape(queries.shape[0], -1), key_terms)

def reference(layer_inputs, keys_values, loss_weight, doc_ids, assignment):
    replicas, micro_count = assignment.shape
    layers = layer_inputs.shape[0]
    features = layer_inputs.shape[-1]
    kv_features = keys_values.shape[-1]
    workers = jnp.arange(replicas, dtype=jnp.int32)
    sources = jax.vmap(lambda worker: source_of(assignment, worker))(workers)
    micro_index = jnp.arange(micro_count, dtype=jnp.int32)
    run_docs = doc_ids[sources, micro_index[None, :]]
    allowed = jax.vmap(jax.vmap(mask_of))(run_docs)
    queries_all = layer_inputs.reshape(layers, replicas, micro_count, SEQ, features)
    kv_home = keys_values.reshape(layers, replicas, micro_count, SEQ, kv_features)
    run_kv = kv_home[:, sources, micro_index[None, :]]
    weights = loss_weight.reshape(replicas, micro_count, SEQ)
    top = layers - 1

    def top_replica(packed):
        return jax.vmap(top_grad)(*packed)
    top_seed = lax.map(top_replica, (queries_all[top], run_kv[top], allowed, weights))

    def layer_step(upstream, inputs_layer):
        layer_queries, layer_kv = inputs_layer

        def one_replica(packed):
            return jax.vmap(tile_backward)(*packed)
        dquery, key_terms = lax.map(one_replica, (layer_queries, layer_kv, allowed, upstream))
        passed = (upstream.astype(jnp.float32) + dquery).astype(jnp.bfloat16)
        return (passed, key_terms.astype(jnp.bfloat16))
    _, result_grads = lax.scan(layer_step, top_seed, (queries_all, run_kv), reverse=True)
    return result_grads.reshape(layers, replicas, micro_count * SEQ, kv_features)
```

```python
import functools

import jax
import jax.numpy as jnp
from jax import lax
from jax.experimental import pallas as pl
from jax.experimental.pallas import tpu as pltpu
from jax.sharding import PartitionSpec as P

MESH = pl.DeviceIdType.MESH
SIDE = 4
REPLICAS = SIDE * SIDE
HEAD = 128
GROUP = 8
MICRO = 8
SEQ = 128
CHUNK = 32
QUARTERS = SEQ // CHUNK
HEADS_HERE = 2
PHASES = HEADS_HERE * QUARTERS
UNITS = PHASES * MICRO
COLUMNS = GROUP * CHUNK
SCALE = HEAD**-0.5
LOG2E = 1.4426950408889634
CHIPS_DEEP = 8
OFFSETS = (
    (2, 2), (2, 1), (1, 2), (2, 3), (3, 2), (1, 1), (3, 3), (1, 3),
    (3, 1), (0, 2), (2, 0), (0, 1), (1, 0), (0, 3), (3, 0),
)


def dot(a, b, contract):
    return lax.dot_general(a, b, ((contract[:1], contract[1:]), ((), ())), preferred_element_type=jnp.float32)


def kernel(assign, q_hbm, kv_hbm, weights, docs, out, *scratch):
    (raw, outgoing, selected, queries, grads_in, grads_out, total, staged, doc_columns, doc_rows, weight_rows) = scratch[:11]
    arriving = scratch[11 : 11 + PHASES]
    (raw_sem, query_own, query_send, query_recv, slot_send, slot_send_twin, slot_recv, grad_send, grad_recv,
     out_own, out_send, out_recv) = scratch[11 + PHASES :]

    section, me = lax.axis_index("section"), lax.axis_index("dp")
    core = lax.rem(section, 2)
    deep = section // 2
    twin = section + 1 - 2 * core
    other = 1 - core
    y, x = me // SIDE, lax.rem(me, SIDE)
    is_top, is_bottom = deep == CHIPS_DEEP - 1, deep == 0

    def replica_at(dy, dx):
        return lax.rem(y + dy, SIDE) * SIDE + lax.rem(x + dx, SIDE)

    load_raw = pltpu.make_async_copy(kv_hbm, raw, raw_sem)
    load_raw.start()
    own_queries = []
    for a in range(HEADS_HERE):
        column = pl.multiple_of((core * HEADS_HERE + a) * GROUP * HEAD, HEAD)
        copy = pltpu.make_async_copy(
            q_hbm.at[:, :, pl.ds(column, GROUP * HEAD)], queries.at[core, a], query_own.at[a]
        )
        copy.start()
        own_queries.append(copy)

    barrier = pltpu.get_barrier_semaphore()
    for dy, dx in OFFSETS:
        for where in (section, twin):
            pl.semaphore_signal(barrier, inc=1, device_id=(where, replica_at(dy, dx)), device_id_type=MESH)
    pl.semaphore_signal(barrier, inc=1, device_id=(twin, me), device_id_type=MESH)

    @pl.when(jnp.logical_not(is_bottom))
    def _():
        pl.semaphore_signal(barrier, inc=1, device_id=(section - 2, me), device_id_type=MESH)

    @pl.when(jnp.logical_not(is_top))
    def _():
        pl.semaphore_signal(barrier, inc=1, device_id=(section + 2, me), device_id_type=MESH)

    given = [assign[me, m] for m in range(MICRO)]
    slot_rows = []
    for k in range(REPLICAS):
        target = replica_at(k // SIDE, k % SIDE)
        row = 0
        for m in range(MICRO):
            row = jnp.where(given[m] == target, m, row)
        slot_rows.append(row)
    sources, slots = [], []
    for m in range(MICRO):
        source = 0
        for s in range(REPLICAS):
            source = jnp.where(assign[s, m] == me, s, source)
        sources.append(source)
        slots.append(
            lax.rem(y - source // SIDE + SIDE, SIDE) * SIDE + lax.rem(x - lax.rem(source, SIDE) + SIDE, SIDE)
        )

    def pack(p):
        a, q = divmod(p, QUARTERS)
        for k in range(REPLICAS):
            for c in range(2):
                for t in range(2):
                    column = (t * 2 * HEADS_HERE + c * HEADS_HERE + a) * HEAD
                    outgoing[p, k, c, :, t * HEAD : (t + 1) * HEAD] = raw[
                        slot_rows[k], q * CHUNK : (q + 1) * CHUNK, column : column + HEAD
                    ]

    def slot_copy(p, k, c, where, target, send_sem):
        return pltpu.make_async_remote_copy(
            src_ref=outgoing.at[p, k, c],
            dst_ref=arriving[p].at[core, k],
            send_sem=send_sem.at[p],
            recv_sem=slot_recv.at[p],
            device_id=(where, target),
            device_id_type=MESH,
        )

    def send(p):
        for dy, dx in OFFSETS:
            for c, where in ((core, section), (other, twin)):
                slot_copy(p, dy * SIDE + dx, c, where, replica_at(dy, dx), slot_send).start()
        slot_copy(p, 0, other, twin, me, slot_send_twin).start()
        pltpu.make_async_copy(outgoing.at[p, 0, core], arriving[p].at[core, 0], slot_recv.at[p]).start()

    def query_copy(a):
        column = pl.multiple_of((other * HEADS_HERE + a) * GROUP * HEAD, HEAD)
        return pltpu.make_async_remote_copy(
            src_ref=q_hbm.at[:, :, pl.ds(column, GROUP * HEAD)],
            dst_ref=queries.at[core, a],
            send_sem=query_send.at[a],
            recv_sem=query_recv.at[a],
            device_id=(twin, me),
            device_id_type=MESH,
        )

    def query_wait(a):
        return pltpu.make_async_remote_copy(
            src_ref=q_hbm.at[:, :, pl.ds(0, GROUP * HEAD)],
            dst_ref=queries.at[other, a],
            send_sem=query_send.at[a],
            recv_sem=query_recv.at[a],
            device_id=(twin, me),
            device_id_type=MESH,
        )

    load_raw.wait()
    pack(0)
    others = 2 * len(OFFSETS) + 1
    pl.semaphore_wait(barrier, others + jnp.where(is_bottom, 0, 1) + jnp.where(is_top, 0, 1))
    send(0)
    query_copy(0).start()
    for p in range(1, 3):
        pack(p)
        send(p)
    query_copy(1).start()

    lane = lax.broadcasted_iota(jnp.int32, (MICRO, SEQ), 1)
    run_docs = jnp.concatenate([docs[sources[m], m : m + 1, :] for m in range(MICRO)], axis=0)
    run_weights = jnp.concatenate([weights[0:1, m * SEQ : (m + 1) * SEQ] for m in range(MICRO)], axis=0)
    for q in range(QUARTERS):
        here = lane // CHUNK == q
        for held, rows in ((run_docs, doc_rows), (run_weights, weight_rows)):
            part = jnp.where(here, held, jnp.zeros_like(held))
            part = part + pltpu.roll(part, CHUNK, 1)
            rows[q] = part + pltpu.roll(part, 2 * CHUNK, 1)
    for m in range(MICRO):
        doc_columns[m] = jnp.broadcast_to(run_docs[m : m + 1], (SEQ, SEQ)).T

    for a in range(HEADS_HERE):
        for q in range(QUARTERS):
            p = a * QUARTERS + q
            if p >= 1 and p + 2 < PHASES:
                pack(p + 2)
                send(p + 2)
            pltpu.make_async_copy(arriving[p], arriving[p], slot_recv.at[p]).wait()
            for m in range(MICRO):
                for b in range(2):
                    selected[b, a, m, q * CHUNK : (q + 1) * CHUNK, :] = arriving[p][b, slots[m]]
            if q == 0:
                own_queries[a].wait()
                query_wait(a).wait_recv()
            first = max(0, q - 2) * CHUNK
            span = (q + 1) * CHUNK - first

            def unit(m, carry, a=a, q=q, p=p, first=first, span=span):
                u = p * MICRO + m
                key_row = lax.broadcasted_iota(jnp.int32, (span, SEQ), 0) + first
                query_row = lax.rem(lax.broadcasted_iota(jnp.int32, (span, SEQ), 1), CHUNK) + q * CHUNK
                same = doc_columns[m, first : first + span, :] == doc_rows[q, pl.ds(m, 1), :]
                bias = jnp.where(same & (key_row <= query_row), 0.0, -1e30)
                bias = jnp.concatenate([bias] * (COLUMNS // SEQ), axis=1)

                units_queries, keys, values, probs = [], [], [], []
                for b in range(2):
                    own = jnp.concatenate(
                        [
                            queries[b, a, m, q * CHUNK : (q + 1) * CHUNK, h * HEAD : (h + 1) * HEAD]
                            for h in range(GROUP)
                        ],
                        axis=0,
                    )
                    key = selected[b, a, m, first : first + span, 0:HEAD]
                    value = selected[b, a, m, first : first + span, HEAD : 2 * HEAD]
                    scores = dot(key, own, (1, 1))
                    soft = jnp.exp2(scores * (SCALE * LOG2E) + bias)
                    prob = soft * (1.0 / jnp.sum(soft, axis=0, keepdims=True))
                    units_queries.append(own)
                    keys.append(key)
                    values.append(value)
                    probs.append(prob)

                @pl.when(is_top)
                def _():
                    b = 1
                    eye = jnp.where(
                        lax.broadcasted_iota(jnp.int32, (HEAD, HEAD), 0)
                        == lax.broadcasted_iota(jnp.int32, (HEAD, HEAD), 1),
                        1.0,
                        0.0,
                    ).astype(jnp.bfloat16)
                    mixed = dot(values[b], probs[b].astype(jnp.bfloat16), (0, 0))
                    flat = dot(eye, units_queries[b], (1, 1))
                    weight = weight_rows[q, pl.ds(m, 1), :]
                    weight = jnp.concatenate([weight] * (COLUMNS // SEQ), axis=1)
                    grads_in[u] = (weight * (flat + mixed)).astype(jnp.bfloat16)

                @pl.when(jnp.logical_not(is_top))
                def _():
                    pltpu.make_async_remote_copy(
                        src_ref=grads_out.at[u],
                        dst_ref=grads_in.at[u],
                        send_sem=grad_send,
                        recv_sem=grad_recv.at[u],
                        device_id=(section, me),
                        device_id_type=MESH,
                    ).wait_recv()

                grads, score_grads = [None, grads_in[u]], [None, None]
                for b in (1, 0):
                    upstream = grads[b]
                    prob_grads = dot(values[b], upstream, (1, 0))
                    delta = jnp.sum(probs[b] * prob_grads, axis=0, keepdims=True)
                    score_grads[b] = (probs[b] * (prob_grads - delta)).astype(jnp.bfloat16)
                    if b == 1:
                        moved = dot(keys[b], score_grads[b], (0, 0)) * SCALE
                        grads[0] = (upstream.astype(jnp.float32) + moved).astype(jnp.bfloat16)

                @pl.when(jnp.logical_not(is_bottom))
                def _():
                    moved = dot(keys[0], score_grads[0], (0, 0)) * SCALE
                    grads_out[u] = (grads[0].astype(jnp.float32) + moved).astype(jnp.bfloat16)
                    pltpu.make_async_remote_copy(
                        src_ref=grads_out.at[u],
                        dst_ref=grads_in.at[u],
                        send_sem=grad_send,
                        recv_sem=grad_recv.at[u],
                        device_id=(section - 2, me),
                        device_id_type=MESH,
                    ).start()

                old = span - CHUNK
                for b in (1, 0):
                    key_term = dot(score_grads[b], units_queries[b], (1, 0)) * SCALE
                    value_term = dot(probs[b].astype(jnp.bfloat16), grads[b], (1, 1))
                    for t, term in ((0, key_term), (1, value_term)):
                        lanes = slice(t * HEAD, (t + 1) * HEAD)
                        if old:
                            total[b, m, first : first + old, lanes] += term[:old]
                        total[b, m, q * CHUNK : (q + 1) * CHUNK, lanes] = term[old:]
                        if q == QUARTERS - 1:
                            staged[b, a, m, t] = total[b, m, :, lanes].astype(jnp.bfloat16)
                if q == QUARTERS - 1:
                    for t in range(2):
                        column = pl.multiple_of((t * 2 * HEADS_HERE + core * HEADS_HERE + a) * HEAD, HEAD)
                        pltpu.make_async_copy(
                            staged.at[core, a, m, t], out.at[m, :, pl.ds(column, HEAD)], out_own
                        ).start()
                        pltpu.make_async_remote_copy(
                            src_ref=staged.at[other, a, m, t],
                            dst_ref=out.at[m, :, pl.ds(column, HEAD)],
                            send_sem=out_send,
                            recv_sem=out_recv,
                            device_id=(twin, me),
                            device_id_type=MESH,
                        ).start()
                return carry

            lax.fori_loop(0, MICRO, unit, 0)

    for p in range(PHASES):
        pltpu.make_async_copy(outgoing.at[p, pl.ds(1, REPLICAS - 1)], outgoing.at[p, pl.ds(1, REPLICAS - 1)], slot_send.at[p]).wait()
        pltpu.make_async_copy(outgoing.at[p, 0, 0], outgoing.at[p, 0, 0], slot_send_twin.at[p]).wait()
    for a in range(HEADS_HERE):
        query_copy(a).wait_send()

    @pl.when(jnp.logical_not(is_bottom))
    def _():
        pltpu.make_async_copy(grads_out, grads_out, grad_send).wait()

    pltpu.make_async_copy(staged.at[0], staged.at[0], out_own).wait()
    pltpu.make_async_copy(staged.at[0], staged.at[0], out_send).wait()
    pltpu.make_async_copy(staged.at[0], staged.at[0], out_recv).wait()


def on_device(layer_inputs, keys_values, loss_weight, doc_ids, assignment):
    features, width = layer_inputs.shape[-1], keys_values.shape[-1]
    bf16, f32, i32 = jnp.bfloat16, jnp.float32, jnp.int32
    dma = pltpu.SemaphoreType.DMA
    whole = pl.BlockSpec(memory_space=pltpu.VMEM)
    remote = pl.BlockSpec(memory_space=pl.ANY)
    grads = pl.pallas_call(
        kernel,
        out_shape=jax.ShapeDtypeStruct((MICRO, SEQ, width), bf16),
        in_specs=[pl.BlockSpec(memory_space=pltpu.SMEM), remote, remote, whole, whole],
        out_specs=remote,
        scratch_shapes=[
            pltpu.VMEM((MICRO, SEQ, width), bf16),
            pltpu.VMEM((PHASES, REPLICAS, 2, CHUNK, 2 * HEAD), bf16),
            pltpu.VMEM((2, HEADS_HERE, MICRO, SEQ, 2 * HEAD), bf16),
            pltpu.VMEM((2, HEADS_HERE, MICRO, SEQ, GROUP * HEAD), bf16),
            pltpu.VMEM((UNITS, HEAD, COLUMNS), bf16),
            pltpu.VMEM((UNITS, HEAD, COLUMNS), bf16),
            pltpu.VMEM((2, MICRO, SEQ, 2 * HEAD), f32),
            pltpu.VMEM((2, HEADS_HERE, MICRO, 2, SEQ, HEAD), bf16),
            pltpu.VMEM((MICRO, SEQ, SEQ), i32),
            pltpu.VMEM((QUARTERS, MICRO, SEQ), i32),
            pltpu.VMEM((QUARTERS, MICRO, SEQ), f32),
            *[pltpu.VMEM((2, REPLICAS, CHUNK, 2 * HEAD), bf16) for _ in range(PHASES)],
            dma,
            dma((HEADS_HERE,)),
            dma((HEADS_HERE,)),
            dma((HEADS_HERE,)),
            dma((PHASES,)),
            dma((PHASES,)),
            dma((PHASES,)),
            dma,
            dma((UNITS,)),
            dma,
            dma,
            dma,
        ],
        compiler_params=pltpu.CompilerParams(
            collective_id=0, has_side_effects=True, vmem_limit_bytes=50 << 20
        ),
    )(
        assignment,
        layer_inputs.reshape(MICRO, SEQ, features),
        keys_values.reshape(MICRO, SEQ, width),
        loss_weight,
        doc_ids,
    )
    return grads.reshape(1, 1, MICRO * SEQ, width)


def solution(mesh):
    placed = (
        P("section", "dp", None, None),
        P("section", "dp", None, None),
        P("dp", None),
        P(),
        P(),
    )
    return jax.shard_map(
        on_device,
        mesh=mesh,
        in_specs=placed,
        out_specs=P("section", "dp", None, None),
        check_vma=False,
    )
```

```python
import functools

import jax
import jax.numpy as jnp
from jax import lax
from jax.experimental import pallas as pl
from jax.experimental.pallas import tpu as pltpu
from jax.sharding import PartitionSpec as P

MESH = pl.DeviceIdType.MESH
SIDE = 4
REPLICAS = SIDE * SIDE
HEAD = 128
GROUP = 8
MICRO = 8
SEQ = 128
HEADS_HERE = 2
BLOCK = 16
REACH = 64
PHASES = ((0, 0, 32), (0, 32, 32), (0, 64, 32), (0, 96, 32), (1, 0, 32), (1, 32, 32), (1, 64, 32), (1, 96, 32))
TOGETHER = 4
AHEAD = 3
BLOCKS = sum(rows // BLOCK for _, _, rows in PHASES) * MICRO
WIDEST = max(rows for _, _, rows in PHASES)
SCALE = HEAD**-0.5
LOG2E = 1.4426950408889634
CHIPS_DEEP = 8
OFFSETS = (
    (2, 2), (2, 1), (1, 2), (2, 3), (3, 2), (1, 1), (3, 3), (1, 3),
    (3, 1), (0, 2), (2, 0), (0, 1), (1, 0), (0, 3), (3, 0),
)


def dot(a, b, contract):
    return lax.dot_general(a, b, ((contract[:1], contract[1:]), ((), ())), preferred_element_type=jnp.float32)


def kernel(assign_hbm, q_hbm, kv_hbm, weights_hbm, docs_hbm, out, *scratch):
    (assign, slot_rows, weights, docs, raw, outgoing, selected, queries, grads_in, grads_out, total, staged, probs_held,
     doc_columns, doc_rows, weight_rows) = scratch[:16]
    arriving = scratch[16 : 16 + len(PHASES)]
    (small_sem, raw_sem, query_own, query_send, query_recv, slot_send, slot_recv, grad_send, grad_recv,
     out_own, out_send, out_recv) = scratch[16 + len(PHASES) :]

    section, me = lax.axis_index("section"), lax.axis_index("dp")
    core = lax.rem(section, 2)
    deep = section // 2
    twin = section + 1 - 2 * core
    other = 1 - core
    y, x = me // SIDE, lax.rem(me, SIDE)
    is_top, is_bottom = deep == CHIPS_DEEP - 1, deep == 0

    def replica_at(dy, dx):
        return lax.rem(y + dy, SIDE) * SIDE + lax.rem(x + dx, SIDE)

    loads = [
        pltpu.make_async_copy(source, held, small_sem.at[i])
        for i, (source, held) in enumerate(((assign_hbm, assign), (weights_hbm, weights), (docs_hbm, docs)))
    ]
    for load in loads:
        load.start()
    load_raw = pltpu.make_async_copy(kv_hbm, raw, raw_sem)
    load_raw.start()
    barrier = pltpu.get_barrier_semaphore()
    for dy, dx in OFFSETS:
        for where in (section, twin):
            pl.semaphore_signal(barrier, inc=1, device_id=(where, replica_at(dy, dx)), device_id_type=MESH)
    pl.semaphore_signal(barrier, inc=1, device_id=(twin, me), device_id_type=MESH)

    @pl.when(jnp.logical_not(is_bottom))
    def _():
        pl.semaphore_signal(barrier, inc=1, device_id=(section - 2, me), device_id_type=MESH)

    @pl.when(jnp.logical_not(is_top))
    def _():
        pl.semaphore_signal(barrier, inc=1, device_id=(section + 2, me), device_id_type=MESH)

    for load in loads:
        load.wait()
    given = [assign[m, me] for m in range(MICRO)]
    for k in range(REPLICAS):
        target = replica_at(k // SIDE, k % SIDE)
        row = 0
        for m in range(MICRO):
            row = jnp.where(given[m] == target, m, row)
        slot_rows[k] = row
    sources, slots = [], []
    for m in range(MICRO):
        source = 0
        for s in range(REPLICAS):
            source = jnp.where(assign[m, s] == me, s, source)
        sources.append(source)
        slots.append(
            lax.rem(y - source // SIDE + SIDE, SIDE) * SIDE + lax.rem(x - lax.rem(source, SIDE) + SIDE, SIDE)
        )

    def pack(p, k):
        a, start, rows = PHASES[p]
        row = slot_rows[k]
        for c in range(2):
            for t in range(2):
                column = (t * 2 * HEADS_HERE + c * HEADS_HERE + a) * HEAD
                outgoing[p, k, c, 0:rows, t * HEAD : (t + 1) * HEAD] = raw[row, start : start + rows, column : column + HEAD]

    def slot_copy(p, k, c, where, target, kind):
        return pltpu.make_async_remote_copy(
            src_ref=outgoing.at[p, k, c, pl.ds(0, PHASES[p][2])],
            dst_ref=arriving[p].at[core, k],
            send_sem=slot_send.at[p, kind],
            recv_sem=slot_recv.at[p],
            device_id=(where, target),
            device_id_type=MESH,
        )

    def keep(p):
        pltpu.make_async_copy(
            outgoing.at[p, 0, core, pl.ds(0, PHASES[p][2])], arriving[p].at[core, 0], slot_recv.at[p]
        ).start()

    def send(p):
        for dy, dx in OFFSETS:
            for c, where in ((core, section), (other, twin)):
                slot_copy(p, dy * SIDE + dx, c, where, replica_at(dy, dx), 0).start()
        slot_copy(p, 0, other, twin, me, 1).start()
        keep(p)

    def send_part(p, m):
        for k in (2 * m, 2 * m + 1):
            pack(p, k)
        for k in (2 * m, 2 * m + 1):
            target = replica_at(k // SIDE, lax.rem(k, SIDE))
            slot_copy(p, k, other, twin, target, jnp.where(k == 0, 1, 0)).start()

            @pl.when(k > 0)
            def _():
                slot_copy(p, k, core, section, target, 0).start()

        @pl.when(m == 0)
        def _():
            keep(p)

    def query_part(p, c):
        a, start, rows = PHASES[p]
        column = pl.multiple_of((c * HEADS_HERE + a) * GROUP * HEAD, HEAD)
        return q_hbm.at[:, pl.ds(start, rows), pl.ds(column, GROUP * HEAD)]

    def query_place(p, b):
        a, start, rows = PHASES[p]
        return queries.at[b, a, :, pl.ds(start, rows)]

    def query_copy(p, b):
        return pltpu.make_async_remote_copy(
            src_ref=query_part(p, other),
            dst_ref=query_place(p, b),
            send_sem=query_send.at[p],
            recv_sem=query_recv.at[p],
            device_id=(twin, me),
            device_id_type=MESH,
        )

    def query_load(p):
        return pltpu.make_async_copy(query_part(p, core), query_place(p, core), query_own.at[p])

    def query_start(p):
        query_load(p).start()
        query_copy(p, core).start()

    load_raw.wait()
    for k in range(REPLICAS):
        pack(0, k)
    others = 2 * len(OFFSETS) + 1
    pl.semaphore_wait(barrier, others + jnp.where(is_bottom, 0, 1) + jnp.where(is_top, 0, 1))
    send(0)
    query_start(0)
    for p in range(1, AHEAD):
        for k in range(REPLICAS):
            pack(p, k)
        send(p)
        query_start(p)

    lane = lax.broadcasted_iota(jnp.int32, (MICRO, SEQ), 1)
    run_docs = jnp.concatenate([docs[sources[m], m : m + 1, :] for m in range(MICRO)], axis=0)
    run_weights = jnp.concatenate([weights[0:1, m * SEQ : (m + 1) * SEQ] for m in range(MICRO)], axis=0)
    for i in range(SEQ // BLOCK):
        here = lane // BLOCK == i
        for held, table in ((run_docs, doc_rows), (run_weights, weight_rows)):
            part = jnp.where(here, held, jnp.zeros_like(held))
            part = pltpu.roll(part, SEQ - i * BLOCK, 1) if i else part
            step = BLOCK
            while step < SEQ:
                part = part + pltpu.roll(part, step, 1)
                step *= 2
            table[i] = part
    for m in range(MICRO):
        doc_columns[m] = jnp.broadcast_to(run_docs[m : m + 1], (SEQ, SEQ)).T

    base = 0
    for p, (a, start, rows) in enumerate(PHASES):
        pltpu.make_async_copy(arriving[p], arriving[p], slot_recv.at[p]).wait()
        for m in range(MICRO):
            for b in range(2):
                selected[b, a, m, start : start + rows, :] = arriving[p][b, slots[m]]
        query_load(p).wait()
        query_copy(p, other).wait_recv()
        if p >= 1 and p + 2 < len(PHASES):
            query_start(p + 2)
        blocks = range(start // BLOCK, (start + rows) // BLOCK)
        first = max(0, (start - REACH + 1) // BLOCK * BLOCK)
        span = start + rows - first
        old = span - rows
        parts = rows // BLOCK
        last = start + rows == SEQ
        done = SEQ if last else max(0, (PHASES[p + 1][1] - REACH + 1) // BLOCK * BLOCK)

        def beside(pieces):
            return jnp.concatenate(pieces, axis=1) if len(pieces) > 1 else pieces[0]

        def queries_of(b, m, a=a, blocks=blocks):
            return jnp.concatenate(
                [
                    queries[b, a, m, i * BLOCK : (i + 1) * BLOCK, h * HEAD : (h + 1) * HEAD]
                    for i in blocks
                    for h in range(GROUP)
                ],
                axis=0,
            )

        def keys_of(b, m, a=a, first=first, span=span):
            return selected[b, a, m, first : first + span, 0:HEAD]

        def values_of(b, m, a=a, first=first, span=span):
            return selected[b, a, m, first : first + span, HEAD : 2 * HEAD]

        def find_probs(m, blocks=blocks, first=first, span=span, rows=rows, beside=beside):
            key_row = lax.broadcasted_iota(jnp.int32, (span, SEQ), 0) + first
            query_row = lax.rem(lax.broadcasted_iota(jnp.int32, (span, SEQ), 1), BLOCK)
            key_docs = doc_columns[m, first : first + span, :]
            masks = [
                jnp.where(
                    (key_docs == doc_rows[i, pl.ds(m, 1), :]) & (key_row <= query_row + i * BLOCK), 0.0, -1e30
                )
                for i in blocks
            ]
            bias = beside(masks)
            for b in (1, 0):
                scores = dot(keys_of(b, m), queries_of(b, m), (1, 1))
                soft = jnp.exp2(scores * (SCALE * LOG2E) + bias)
                prob = soft * (1.0 / jnp.sum(soft, axis=0, keepdims=True))
                probs_held[lax.rem(m, 2), b, 0:span, 0 : GROUP * rows] = prob

        def unit(m, carry, p=p, a=a, start=start, rows=rows, span=span, first=first, old=old, parts=parts, last=last, done=done,
                 base=base, blocks=blocks, beside=beside):
            at = base + m * parts

            def grad_copy(where):
                return pltpu.make_async_remote_copy(
                    src_ref=grads_out.at[pl.ds(at, parts)],
                    dst_ref=grads_in.at[pl.ds(at, parts)],
                    send_sem=grad_send,
                    recv_sem=grad_recv.at[p, m],
                    device_id=(where, me),
                    device_id_type=MESH,
                )

            def put(ref, value):
                for i in range(parts):
                    ref[at + i] = value[:, i * SEQ : (i + 1) * SEQ]

            probs = [probs_held[lax.rem(m, 2), b, 0:span, 0 : GROUP * rows] for b in range(2)]

            @pl.when(is_top)
            def _():
                eye = jnp.where(
                    lax.broadcasted_iota(jnp.int32, (HEAD, HEAD), 0)
                    == lax.broadcasted_iota(jnp.int32, (HEAD, HEAD), 1),
                    1.0,
                    0.0,
                ).astype(jnp.bfloat16)
                mixed = dot(values_of(1, m), probs[1].astype(jnp.bfloat16), (0, 0))
                flat = dot(eye, queries_of(1, m), (1, 1))
                weight = beside([weight_rows[i, pl.ds(m, 1), :] for i in blocks])
                put(grads_in, (weight * (flat + mixed)).astype(jnp.bfloat16))

            @pl.when(jnp.logical_not(is_top))
            def _():
                grad_copy(section).wait_recv()

            upstream = beside([grads_in[at + i] for i in range(parts)])
            grads, score_grads = [None, upstream], [None, None]
            for b in (1, 0):
                prob = probs[b]
                prob_grads = dot(values_of(b, m), grads[b], (1, 0))
                delta = jnp.sum(prob * prob_grads, axis=0, keepdims=True)
                score_grads[b] = (prob * (prob_grads - delta)).astype(jnp.bfloat16)
                if b == 1:
                    moved = dot(keys_of(b, m), score_grads[b], (0, 0)) * SCALE
                    grads[0] = (upstream.astype(jnp.float32) + moved).astype(jnp.bfloat16)

            @pl.when(jnp.logical_not(is_bottom))
            def _():
                moved = dot(keys_of(0, m), score_grads[0], (0, 0)) * SCALE
                put(grads_out, (grads[0].astype(jnp.float32) + moved).astype(jnp.bfloat16))
                grad_copy(section - 2).start()

            for b in (1, 0):
                key_term = dot(score_grads[b], queries_of(b, m), (1, 0)) * SCALE
                value_term = dot(probs[b].astype(jnp.bfloat16), grads[b], (1, 1))
                for t, term in ((0, key_term), (1, value_term)):
                    lanes = slice(t * HEAD, (t + 1) * HEAD)
                    for low, high, seen in ((first, start, True), (start, start + rows, False)):
                        for begin, end, final in ((low, min(high, done), True), (max(low, done), high, False)):
                            if begin < end:
                                piece = term[begin - first : end - first]
                                if seen:
                                    piece = piece + total[b, m, begin:end, lanes]
                                if final:
                                    staged[b, a, t, m, begin:end] = piece.astype(jnp.bfloat16)
                                else:
                                    total[b, m, begin:end, lanes] = piece
            find_probs(jnp.minimum(m + 1, MICRO - 1))
            if last:

                @pl.when(lax.rem(m, TOGETHER) == TOGETHER - 1)
                def _():
                    some = pl.ds(m - (TOGETHER - 1), TOGETHER)
                    for t in range(2):
                        column = pl.multiple_of((t * 2 * HEADS_HERE + core * HEADS_HERE + a) * HEAD, HEAD)
                        place = out.at[some, :, pl.ds(column, HEAD)]
                        pltpu.make_async_copy(staged.at[core, a, t, some], place, out_own).start()
                        pltpu.make_async_remote_copy(
                            src_ref=staged.at[other, a, t, some],
                            dst_ref=place,
                            send_sem=out_send,
                            recv_sem=out_recv,
                            device_id=(twin, me),
                            device_id_type=MESH,
                        ).start()
            if p >= 1 and p + 2 < len(PHASES):
                send_part(p + 2, m)
            return carry

        find_probs(0)
        lax.fori_loop(0, MICRO, unit, 0)
        base += parts * MICRO

    for p, (_, _, rows) in enumerate(PHASES):
        for i, part in enumerate(
            (outgoing.at[p, pl.ds(1, REPLICAS - 1), :, pl.ds(0, rows)], outgoing.at[p, 0, 0, pl.ds(0, rows)])
        ):
            pltpu.make_async_copy(part, part, slot_send.at[p, i]).wait()
    for p in range(len(PHASES)):
        query_copy(p, core).wait_send()

    @pl.when(jnp.logical_not(is_bottom))
    def _():
        pltpu.make_async_copy(grads_out, grads_out, grad_send).wait()

    pltpu.make_async_copy(staged.at[0], staged.at[0], out_own).wait()
    pltpu.make_async_copy(staged.at[0], staged.at[0], out_send).wait()
    pltpu.make_async_copy(staged.at[0], staged.at[0], out_recv).wait()


def on_device(layer_inputs, keys_values, loss_weight, doc_ids, assignment):
    features, width = layer_inputs.shape[-1], keys_values.shape[-1]
    bf16, f32, i32 = jnp.bfloat16, jnp.float32, jnp.int32
    dma = pltpu.SemaphoreType.DMA
    remote = pl.BlockSpec(memory_space=pl.ANY)
    grads = pl.pallas_call(
        kernel,
        out_shape=jax.ShapeDtypeStruct((MICRO, SEQ, width), bf16),
        in_specs=[remote] * 5,
        out_specs=remote,
        scratch_shapes=[
            pltpu.SMEM((MICRO, REPLICAS), i32),
            pltpu.SMEM((REPLICAS,), i32),
            pltpu.VMEM((1, MICRO * SEQ), f32),
            pltpu.VMEM((REPLICAS, MICRO, SEQ), i32),
            pltpu.VMEM((MICRO, SEQ, width), bf16),
            pltpu.VMEM((len(PHASES), REPLICAS, 2, WIDEST, 2 * HEAD), bf16),
            pltpu.VMEM((2, HEADS_HERE, MICRO, SEQ, 2 * HEAD), bf16),
            pltpu.VMEM((2, HEADS_HERE, MICRO, SEQ, GROUP * HEAD), bf16),
            pltpu.VMEM((BLOCKS, HEAD, SEQ), bf16),
            pltpu.VMEM((BLOCKS, HEAD, SEQ), bf16),
            pltpu.VMEM((2, MICRO, SEQ, 2 * HEAD), f32),
            pltpu.VMEM((2, HEADS_HERE, 2, MICRO, SEQ, HEAD), bf16),
            pltpu.VMEM((2, 2, SEQ, GROUP * WIDEST), f32),
            pltpu.VMEM((MICRO, SEQ, SEQ), i32),
            pltpu.VMEM((SEQ // BLOCK, MICRO, SEQ), i32),
            pltpu.VMEM((SEQ // BLOCK, MICRO, SEQ), f32),
            *[pltpu.VMEM((2, REPLICAS, rows, 2 * HEAD), bf16) for _, _, rows in PHASES],
            dma((3,)),
            dma,
            dma((len(PHASES),)),
            dma((len(PHASES),)),
            dma((len(PHASES),)),
            dma((len(PHASES), 2)),
            dma((len(PHASES),)),
            dma,
            dma((len(PHASES), MICRO)),
            dma,
            dma,
            dma,
        ],
        compiler_params=pltpu.CompilerParams(
            collective_id=0, has_side_effects=True, vmem_limit_bytes=50 << 20
        ),
    )(
        pltpu.with_memory_space_constraint(assignment.T, pltpu.HBM),
        layer_inputs.reshape(MICRO, SEQ, features),
        keys_values.reshape(MICRO, SEQ, width),
        pltpu.with_memory_space_constraint(loss_weight, pltpu.HBM),
        pltpu.with_memory_space_constraint(doc_ids, pltpu.HBM),
    )
    return grads.reshape(1, 1, MICRO * SEQ, width)


def solution(mesh):
    placed = (
        P("section", "dp", None, None),
        P("section", "dp", None, None),
        P("dp", None),
        P(),
        P(),
    )
    return jax.shard_map(
        on_device,
        mesh=mesh,
        in_specs=placed,
        out_specs=P("section", "dp", None, None),
        check_vma=False,
    )
```

```python
import functools

import jax
import jax.numpy as jnp
from jax import lax
from jax.experimental import pallas as pl
from jax.experimental.pallas import tpu as pltpu
from jax.sharding import PartitionSpec as P

MESH = pl.DeviceIdType.MESH
SIDE = 4
REPLICAS = SIDE * SIDE
HEAD = 128
GROUP = 8
MICRO = 8
SEQ = 128
HEADS_HERE = 2
BLOCK = 16
REACH = 64
PHASES = ((0, 0, 32), (0, 32, 32), (0, 64, 32), (0, 96, 32), (1, 0, 32), (1, 32, 32), (1, 64, 32), (1, 96, 32))
TOGETHER = 4
AHEAD = 2
BLOCKS = sum(rows // BLOCK for _, _, rows in PHASES) * MICRO
WIDEST = max(rows for _, _, rows in PHASES)
SCALE = HEAD**-0.5
LOG2E = 1.4426950408889634
CHIPS_DEEP = 8
OFFSETS = (
    (2, 2), (2, 1), (1, 2), (2, 3), (3, 2), (1, 1), (3, 3), (1, 3),
    (3, 1), (0, 2), (2, 0), (0, 1), (1, 0), (0, 3), (3, 0),
)


def dot(a, b, contract):
    return lax.dot_general(a, b, ((contract[:1], contract[1:]), ((), ())), preferred_element_type=jnp.float32)


def kernel(assign_hbm, q_hbm, kv_hbm, weights_hbm, docs_hbm, out, *scratch):
    (assign, slot_rows, weights, docs, raw, outgoing, selected, queries, grads_in, grads_out, total, staged, probs_held,
     doc_columns, doc_rows, weight_rows) = scratch[:16]
    arriving = scratch[16 : 16 + len(PHASES)]
    (small_sem, raw_sem, query_own, query_send, query_recv, slot_send, slot_recv, grad_send, grad_recv,
     out_own, out_send, out_recv) = scratch[16 + len(PHASES) :]

    section, me = lax.axis_index("section"), lax.axis_index("dp")
    core = lax.rem(section, 2)
    deep = section // 2
    twin = section + 1 - 2 * core
    other = 1 - core
    y, x = me // SIDE, lax.rem(me, SIDE)
    is_top, is_bottom = deep == CHIPS_DEEP - 1, deep == 0

    def replica_at(dy, dx):
        return lax.rem(y + dy, SIDE) * SIDE + lax.rem(x + dx, SIDE)

    loads = [
        pltpu.make_async_copy(source, held, small_sem.at[i])
        for i, (source, held) in enumerate(((assign_hbm, assign), (weights_hbm, weights), (docs_hbm, docs)))
    ]
    for load in loads:
        load.start()
    load_raw = pltpu.make_async_copy(kv_hbm, raw, raw_sem)
    load_raw.start()
    barrier = pltpu.get_barrier_semaphore()
    for dy, dx in OFFSETS:
        for where in (section, twin):
            pl.semaphore_signal(barrier, inc=1, device_id=(where, replica_at(dy, dx)), device_id_type=MESH)
    pl.semaphore_signal(barrier, inc=1, device_id=(twin, me), device_id_type=MESH)

    @pl.when(jnp.logical_not(is_bottom))
    def _():
        pl.semaphore_signal(barrier, inc=1, device_id=(section - 2, me), device_id_type=MESH)

    @pl.when(jnp.logical_not(is_top))
    def _():
        pl.semaphore_signal(barrier, inc=1, device_id=(section + 2, me), device_id_type=MESH)

    loads[0].wait()
    given = [assign[m, me] for m in range(MICRO)]
    for k in range(REPLICAS):
        target = replica_at(k // SIDE, k % SIDE)
        row = 0
        for m in range(MICRO):
            row = jnp.where(given[m] == target, m, row)
        slot_rows[k] = row

    def pack(p, k):
        a, start, rows = PHASES[p]
        row = slot_rows[k]
        for c in range(2):
            for t in range(2):
                column = (t * 2 * HEADS_HERE + c * HEADS_HERE + a) * HEAD
                outgoing[p, k, c, 0:rows, t * HEAD : (t + 1) * HEAD] = raw[row, start : start + rows, column : column + HEAD]

    def slot_copy(p, k, c, where, target, kind):
        return pltpu.make_async_remote_copy(
            src_ref=outgoing.at[p, k, c, pl.ds(0, PHASES[p][2])],
            dst_ref=arriving[p].at[core, k],
            send_sem=slot_send.at[p, kind],
            recv_sem=slot_recv.at[p],
            device_id=(where, target),
            device_id_type=MESH,
        )

    def keep(p):
        pltpu.make_async_copy(
            outgoing.at[p, 0, core, pl.ds(0, PHASES[p][2])], arriving[p].at[core, 0], slot_recv.at[p]
        ).start()

    def send(p):
        for dy, dx in OFFSETS:
            for c, where in ((core, section), (other, twin)):
                slot_copy(p, dy * SIDE + dx, c, where, replica_at(dy, dx), 0).start()
        slot_copy(p, 0, other, twin, me, 1).start()
        keep(p)

    def send_part(p, m):
        for k in (2 * m, 2 * m + 1):
            pack(p, k)
        for k in (2 * m, 2 * m + 1):
            target = replica_at(k // SIDE, lax.rem(k, SIDE))
            slot_copy(p, k, other, twin, target, jnp.where(k == 0, 1, 0)).start()

            @pl.when(k > 0)
            def _():
                slot_copy(p, k, core, section, target, 0).start()

        @pl.when(m == 0)
        def _():
            keep(p)

    def query_part(p, c):
        a, start, rows = PHASES[p]
        column = pl.multiple_of((c * HEADS_HERE + a) * GROUP * HEAD, HEAD)
        return q_hbm.at[:, pl.ds(start, rows), pl.ds(column, GROUP * HEAD)]

    def query_place(p, b):
        a, start, rows = PHASES[p]
        return queries.at[b, a, :, pl.ds(start, rows)]

    def query_copy(p, b):
        return pltpu.make_async_remote_copy(
            src_ref=query_part(p, other),
            dst_ref=query_place(p, b),
            send_sem=query_send.at[p],
            recv_sem=query_recv.at[p],
            device_id=(twin, me),
            device_id_type=MESH,
        )

    def query_load(p):
        return pltpu.make_async_copy(query_part(p, core), query_place(p, core), query_own.at[p])

    def query_start(p):
        query_load(p).start()
        query_copy(p, core).start()

    load_raw.wait()
    for k in range(REPLICAS):
        pack(0, k)
    others = 2 * len(OFFSETS) + 1
    pl.semaphore_wait(barrier, others + jnp.where(is_bottom, 0, 1) + jnp.where(is_top, 0, 1))
    send(0)
    query_start(0)
    for p in range(1, AHEAD):
        for k in range(REPLICAS):
            pack(p, k)
        send(p)
        query_start(p)

    for load in loads[1:]:
        load.wait()
    sources, slots = [], []
    for m in range(MICRO):
        source = 0
        for s in range(REPLICAS):
            source = jnp.where(assign[m, s] == me, s, source)
        sources.append(source)
        slots.append(
            lax.rem(y - source // SIDE + SIDE, SIDE) * SIDE + lax.rem(x - lax.rem(source, SIDE) + SIDE, SIDE)
        )

    lane = lax.broadcasted_iota(jnp.int32, (MICRO, SEQ), 1)
    run_docs = jnp.concatenate([docs[sources[m], m : m + 1, :] for m in range(MICRO)], axis=0)
    run_weights = jnp.concatenate([weights[0:1, m * SEQ : (m + 1) * SEQ] for m in range(MICRO)], axis=0)
    for i in range(SEQ // BLOCK):
        here = lane // BLOCK == i
        for held, table in ((run_docs, doc_rows), (run_weights, weight_rows)):
            part = jnp.where(here, held, jnp.zeros_like(held))
            part = pltpu.roll(part, SEQ - i * BLOCK, 1) if i else part
            step = BLOCK
            while step < SEQ:
                part = part + pltpu.roll(part, step, 1)
                step *= 2
            table[i] = part
    for m in range(MICRO):
        doc_columns[m] = jnp.broadcast_to(run_docs[m : m + 1], (SEQ, SEQ)).T

    base = 0
    for p, (a, start, rows) in enumerate(PHASES):
        pltpu.make_async_copy(arriving[p], arriving[p], slot_recv.at[p]).wait()
        for m in range(MICRO):
            for b in range(2):
                selected[b, a, m, start : start + rows, :] = arriving[p][b, slots[m]]
        query_load(p).wait()
        query_copy(p, other).wait_recv()
        if p + 2 < len(PHASES):
            query_start(p + 2)
        blocks = range(start // BLOCK, (start + rows) // BLOCK)
        first = max(0, (start - REACH + 1) // BLOCK * BLOCK)
        span = start + rows - first
        old = span - rows
        parts = rows // BLOCK
        last = start + rows == SEQ
        done = SEQ if last else max(0, (PHASES[p + 1][1] - REACH + 1) // BLOCK * BLOCK)

        def beside(pieces):
            return jnp.concatenate(pieces, axis=1) if len(pieces) > 1 else pieces[0]

        def queries_of(b, m, a=a, blocks=blocks):
            return jnp.concatenate(
                [
                    queries[b, a, m, i * BLOCK : (i + 1) * BLOCK, h * HEAD : (h + 1) * HEAD]
                    for i in blocks
                    for h in range(GROUP)
                ],
                axis=0,
            )

        def keys_of(b, m, a=a, first=first, span=span):
            return selected[b, a, m, first : first + span, 0:HEAD]

        def values_of(b, m, a=a, first=first, span=span):
            return selected[b, a, m, first : first + span, HEAD : 2 * HEAD]

        def find_probs(m, blocks=blocks, first=first, span=span, rows=rows, beside=beside):
            key_row = lax.broadcasted_iota(jnp.int32, (span, SEQ), 0) + first
            query_row = lax.rem(lax.broadcasted_iota(jnp.int32, (span, SEQ), 1), BLOCK)
            key_docs = doc_columns[m, first : first + span, :]
            masks = [
                jnp.where(
                    (key_docs == doc_rows[i, pl.ds(m, 1), :]) & (key_row <= query_row + i * BLOCK), 0.0, -1e30
                )
                for i in blocks
            ]
            bias = beside(masks)
            for b in (1, 0):
                scores = dot(keys_of(b, m), queries_of(b, m), (1, 1))
                soft = jnp.exp2(scores * (SCALE * LOG2E) + bias)
                prob = soft * (1.0 / jnp.sum(soft, axis=0, keepdims=True))
                probs_held[lax.rem(m, 2), b, 0:span, 0 : GROUP * rows] = prob

        def unit(m, carry, p=p, a=a, start=start, rows=rows, span=span, first=first, old=old, parts=parts, last=last, done=done,
                 base=base, blocks=blocks, beside=beside):
            at = base + m * parts

            def grad_copy(where):
                return pltpu.make_async_remote_copy(
                    src_ref=grads_out.at[pl.ds(at, parts)],
                    dst_ref=grads_in.at[pl.ds(at, parts)],
                    send_sem=grad_send,
                    recv_sem=grad_recv.at[p, m],
                    device_id=(where, me),
                    device_id_type=MESH,
                )

            def put(ref, value):
                for i in range(parts):
                    ref[at + i] = value[:, i * SEQ : (i + 1) * SEQ]

            probs = [probs_held[lax.rem(m, 2), b, 0:span, 0 : GROUP * rows] for b in range(2)]

            @pl.when(is_top)
            def _():
                eye = jnp.where(
                    lax.broadcasted_iota(jnp.int32, (HEAD, HEAD), 0)
                    == lax.broadcasted_iota(jnp.int32, (HEAD, HEAD), 1),
                    1.0,
                    0.0,
                ).astype(jnp.bfloat16)
                mixed = dot(values_of(1, m), probs[1].astype(jnp.bfloat16), (0, 0))
                flat = dot(eye, queries_of(1, m), (1, 1))
                weight = beside([weight_rows[i, pl.ds(m, 1), :] for i in blocks])
                put(grads_in, (weight * (flat + mixed)).astype(jnp.bfloat16))

            @pl.when(jnp.logical_not(is_top))
            def _():
                grad_copy(section).wait_recv()

            upstream = beside([grads_in[at + i] for i in range(parts)])
            grads, score_grads = [None, upstream], [None, None]
            for b in (1, 0):
                prob = probs[b]
                prob_grads = dot(values_of(b, m), grads[b], (1, 0))
                delta = jnp.sum(prob * prob_grads, axis=0, keepdims=True)
                score_grads[b] = (prob * (prob_grads - delta)).astype(jnp.bfloat16)
                if b == 1:
                    moved = dot(keys_of(b, m), score_grads[b], (0, 0)) * SCALE
                    grads[0] = (upstream.astype(jnp.float32) + moved).astype(jnp.bfloat16)

            @pl.when(jnp.logical_not(is_bottom))
            def _():
                moved = dot(keys_of(0, m), score_grads[0], (0, 0)) * SCALE
                put(grads_out, (grads[0].astype(jnp.float32) + moved).astype(jnp.bfloat16))
                grad_copy(section - 2).start()

            for b in (1, 0):
                key_term = dot(score_grads[b], queries_of(b, m), (1, 0)) * SCALE
                value_term = dot(probs[b].astype(jnp.bfloat16), grads[b], (1, 1))
                for t, term in ((0, key_term), (1, value_term)):
                    lanes = slice(t * HEAD, (t + 1) * HEAD)
                    for low, high, seen in ((first, start, True), (start, start + rows, False)):
                        for begin, end, final in ((low, min(high, done), True), (max(low, done), high, False)):
                            if begin < end:
                                piece = term[begin - first : end - first]
                                if seen:
                                    piece = piece + total[b, m, begin:end, lanes]
                                if final:
                                    staged[b, a, t, m, begin:end] = piece.astype(jnp.bfloat16)
                                else:
                                    total[b, m, begin:end, lanes] = piece
            find_probs(jnp.minimum(m + 1, MICRO - 1))
            if last:

                @pl.when(lax.rem(m, TOGETHER) == TOGETHER - 1)
                def _():
                    some = pl.ds(m - (TOGETHER - 1), TOGETHER)
                    for t in range(2):
                        column = pl.multiple_of((t * 2 * HEADS_HERE + core * HEADS_HERE + a) * HEAD, HEAD)
                        place = out.at[some, :, pl.ds(column, HEAD)]
                        pltpu.make_async_copy(staged.at[core, a, t, some], place, out_own).start()
                        pltpu.make_async_remote_copy(
                            src_ref=staged.at[other, a, t, some],
                            dst_ref=place,
                            send_sem=out_send,
                            recv_sem=out_recv,
                            device_id=(twin, me),
                            device_id_type=MESH,
                        ).start()
            if p + 2 < len(PHASES):
                send_part(p + 2, m)
            return carry

        find_probs(0)
        lax.fori_loop(0, MICRO, unit, 0)
        base += parts * MICRO

    for p, (_, _, rows) in enumerate(PHASES):
        for i, part in enumerate(
            (outgoing.at[p, pl.ds(1, REPLICAS - 1), :, pl.ds(0, rows)], outgoing.at[p, 0, 0, pl.ds(0, rows)])
        ):
            pltpu.make_async_copy(part, part, slot_send.at[p, i]).wait()
    for p in range(len(PHASES)):
        query_copy(p, core).wait_send()

    @pl.when(jnp.logical_not(is_bottom))
    def _():
        pltpu.make_async_copy(grads_out, grads_out, grad_send).wait()

    pltpu.make_async_copy(staged.at[0], staged.at[0], out_own).wait()
    pltpu.make_async_copy(staged.at[0], staged.at[0], out_send).wait()
    pltpu.make_async_copy(staged.at[0], staged.at[0], out_recv).wait()


def on_device(layer_inputs, keys_values, loss_weight, doc_ids, assignment):
    features, width = layer_inputs.shape[-1], keys_values.shape[-1]
    bf16, f32, i32 = jnp.bfloat16, jnp.float32, jnp.int32
    dma = pltpu.SemaphoreType.DMA
    remote = pl.BlockSpec(memory_space=pl.ANY)
    grads = pl.pallas_call(
        kernel,
        out_shape=jax.ShapeDtypeStruct((MICRO, SEQ, width), bf16),
        in_specs=[remote] * 5,
        out_specs=remote,
        scratch_shapes=[
            pltpu.SMEM((MICRO, REPLICAS), i32),
            pltpu.SMEM((REPLICAS,), i32),
            pltpu.VMEM((1, MICRO * SEQ), f32),
            pltpu.VMEM((REPLICAS, MICRO, SEQ), i32),
            pltpu.VMEM((MICRO, SEQ, width), bf16),
            pltpu.VMEM((len(PHASES), REPLICAS, 2, WIDEST, 2 * HEAD), bf16),
            pltpu.VMEM((2, HEADS_HERE, MICRO, SEQ, 2 * HEAD), bf16),
            pltpu.VMEM((2, HEADS_HERE, MICRO, SEQ, GROUP * HEAD), bf16),
            pltpu.VMEM((BLOCKS, HEAD, SEQ), bf16),
            pltpu.VMEM((BLOCKS, HEAD, SEQ), bf16),
            pltpu.VMEM((2, MICRO, SEQ, 2 * HEAD), f32),
            pltpu.VMEM((2, HEADS_HERE, 2, MICRO, SEQ, HEAD), bf16),
            pltpu.VMEM((2, 2, SEQ, GROUP * WIDEST), f32),
            pltpu.VMEM((MICRO, SEQ, SEQ), i32),
            pltpu.VMEM((SEQ // BLOCK, MICRO, SEQ), i32),
            pltpu.VMEM((SEQ // BLOCK, MICRO, SEQ), f32),
            *[pltpu.VMEM((2, REPLICAS, rows, 2 * HEAD), bf16) for _, _, rows in PHASES],
            dma((3,)),
            dma,
            dma((len(PHASES),)),
            dma((len(PHASES),)),
            dma((len(PHASES),)),
            dma((len(PHASES), 2)),
            dma((len(PHASES),)),
            dma,
            dma((len(PHASES), MICRO)),
            dma,
            dma,
            dma,
        ],
        compiler_params=pltpu.CompilerParams(
            collective_id=0, has_side_effects=True, vmem_limit_bytes=50 << 20
        ),
    )(
        pltpu.with_memory_space_constraint(assignment.T, pltpu.HBM),
        layer_inputs.reshape(MICRO, SEQ, features),
        keys_values.reshape(MICRO, SEQ, width),
        pltpu.with_memory_space_constraint(loss_weight, pltpu.HBM),
        pltpu.with_memory_space_constraint(doc_ids, pltpu.HBM),
    )
    return grads.reshape(1, 1, MICRO * SEQ, width)


def solution(mesh):
    placed = (
        P("section", "dp", None, None),
        P("section", "dp", None, None),
        P("dp", None),
        P(),
        P(),
    )
    return jax.shard_map(
        on_device,
        mesh=mesh,
        in_specs=placed,
        out_specs=P("section", "dp", None, None),
        check_vma=False,
    )
```
